32 devices in a mesh: seq: 8 (over z, core), chan: 4 (over y, x).
Axes of the slice: x: 2, y: 2, z: 4, core: 2. Of those that a mesh axis runs over, the one named last changes fastest.
Arguments:
- features: bfloat16 [3, 4096, 4096], P(None, ('seq', 'chan')), may hold values from -6 to 6
- short_weight: float32 [3, 3, 4096], replicated, may hold values from -3.5 to 3.5
- decay_rate: float32 [16, 4096], P(None, 'chan'), as said below
- residue: float32 [16, 4096], P(None, 'chan'), may hold values from -1.5 to 1.5
- skip_gain: float32 [4096], P('chan'), may hold values from 0.5 to 1.5
Outputs:
- mixed: bfloat16 [4096, 4096], P(('seq', 'chan'))
The draws below stay inside these ranges and needn't reach their ends.
Inputs may be any that keep to these rules, and one draw needn't show every extreme that they name: `decay_rate`: every rate is positive and at most 1/30.
All inputs are finite; a program needn't handle non-finite values.
Results may differ from the reference program's by a relative error of at most 0.0075.
Values may be sent and summed in bfloat16 or wider, within the bound.
A program may use at most 128 MiB of HBM per device.

```python
import math
import jax
import jax.numpy as jnp
from jax import lax

D = 4096
STATE = 16
SHORT = 3
TOKENS = 4096


def draw_decay_rate(key, part):
    first_key, second_key, third_key = jax.random.split(key, 3)
    share = 0.5
    slow_rates = jnp.exp(jax.random.uniform(second_key, (STATE, D), jnp.float32, math.log(0.2 / TOKENS), math.log(2.0 / TOKENS)))
    quick_rates = jnp.exp(jax.random.uniform(third_key, (STATE, D), jnp.float32, math.log(2.0 / TOKENS), math.log(1.0 / 30.0)))
    chosen = jax.random.uniform(first_key, (STATE, D), jnp.float32) < share
    return jnp.where(chosen, slow_rates, quick_rates)


def shard_levels(own_key, extent, cuts, smallest, high):
    def one(position, shards_of):
        draws = jax.random.uniform(jax.random.fold_in(jax.random.fold_in(own_key, 6), position), (shards_of,), jnp.float32, smallest / len(cuts), high / len(cuts))
        return jnp.repeat(jnp.exp(draws), extent[position] // shards_of).reshape((-1,) + (1,) * (len(extent) - position - 1))

    gain = one(*cuts[0])
    for cut in cuts[1:]:
        gain = gain * one(*cut)
    return gain


def normal_values(rng, extent, spread, reach, shards=(), held_as=jnp.bfloat16):
    result = spread * jax.random.normal(rng, extent, jnp.float32)
    if shards:
        result = result * shard_levels(rng, extent, shards, -0.22, 0.18)
    return jnp.clip(result, -reach, reach).astype(held_as)


def setup_inputs(seed: int = 0) -> dict:
    arg_keys = jax.random.split(jax.random.key(seed), 6)
    features = normal_values(arg_keys[0], (3, TOKENS, D), 1.0, 6.0, ((1, 32),))
    short_weight = normal_values(arg_keys[1], (3, SHORT, D), SHORT ** -0.5, 3.5, (), jnp.float32)
    decay_rate = draw_decay_rate(jax.random.fold_in(arg_keys[5], 71), 0)
    residue = normal_values(arg_keys[3], (STATE, D), 0.25, 1.5, ((1, 4),), jnp.float32)
    skip_gain = jnp.clip(0.5 + 1.0 * jax.random.uniform(arg_keys[4], (D,), jnp.float32) ** shard_levels(arg_keys[4], (D,), ((0, 4),), -0.2, 0.2), 0.5, 1.5)
    return dict(features=features, short_weight=short_weight, decay_rate=decay_rate, residue=residue, skip_gain=skip_gain)


block_len = 128

def short_filter(padded, weights, taps):
    length = padded.shape[1] - taps + 1
    total = jnp.zeros((padded.shape[0], length, padded.shape[2]), jnp.float32)
    for offset in range(taps):
        window = lax.slice_in_dim(padded, taps - 1 - offset, taps - 1 - offset + length, axis=1).astype(jnp.float32)
        total = total + weights[:, offset, :][:, None, :] * window
    return total

def modal_tables(decay_rate, scaled_residue, block):
    positions = jnp.arange(block).astype(jnp.float32)
    kernel = lax.optimization_barrier(jnp.sum(scaled_residue[:, None, :] * jnp.exp(-decay_rate[:, None, :] * positions[None, :, None]), axis=0))
    lag_index = (jnp.arange(block)[:, None] - jnp.arange(block)[None, :]).astype(jnp.int32)
    toeplitz = jnp.where((lag_index >= 0)[:, :, None], kernel[jnp.clip(lag_index, 0, block - 1)], jnp.zeros((), jnp.float32))
    ending = jnp.exp(-decay_rate[:, None, :] * (block - 1.0 - positions)[None, :, None])
    reading = scaled_residue[:, None, :] * jnp.exp(-decay_rate[:, None, :] * (positions + 1.0)[None, :, None])
    return (toeplitz, ending, reading)

def modal_conv(signal, decay_rate, tables, start_state, block):
    toeplitz, ending, reading = tables
    count = signal.shape[0] // block
    pieces = signal.reshape(count, block, signal.shape[1])
    inner = jnp.einsum('ijc,kjc->kic', toeplitz, pieces, precision=lax.Precision.HIGHEST)
    local_end = jnp.einsum('njc,kjc->knc', ending, pieces, precision=lax.Precision.HIGHEST)
    group_decay = jnp.exp(-decay_rate * block)

    def advance(state, piece):
        return (group_decay * state + piece, state)
    final, starts = lax.scan(advance, start_state, local_end)
    carried = jnp.einsum('nic,knc->kic', reading, starts, precision=lax.Precision.HIGHEST)
    return ((inner + carried).reshape(signal.shape), final)

def reference(features, short_weight, decay_rate, residue, skip_gain):
    width = math.gcd(D, 128)
    count = D // width
    block = math.gcd(TOKENS, block_len)

    def one_block(index):
        first = (index * width).astype(jnp.int32)
        streams = lax.dynamic_slice_in_dim(features, first, width, 2)
        weights = lax.dynamic_slice_in_dim(short_weight, first, width, 2)
        rates = lax.dynamic_slice_in_dim(decay_rate, first, width, 1)
        modes = lax.dynamic_slice_in_dim(residue, first, width, 1)
        skips = lax.dynamic_slice_in_dim(skip_gain, first, width, 0)
        padded = jnp.concatenate([jnp.zeros((3, SHORT - 1, width), features.dtype), streams], axis=1)
        filtered = lax.optimization_barrier(short_filter(padded, weights, SHORT).astype(jnp.bfloat16))
        product = lax.optimization_barrier((filtered[1].astype(jnp.float32) * filtered[2].astype(jnp.float32)).astype(jnp.bfloat16))
        signal = product.astype(jnp.float32)
        scaled = modes * jnp.sqrt(1.0 - jnp.exp(-2.0 * rates))
        tables = modal_tables(rates, scaled, block)
        longconv, unused_end = modal_conv(signal, rates, tables, jnp.zeros_like(rates), block)
        conv_out = lax.optimization_barrier((longconv + skips[None, :] * signal).astype(jnp.bfloat16))
        return (filtered[0].astype(jnp.float32) * conv_out.astype(jnp.float32)).astype(jnp.bfloat16)
    stacked = lax.map(one_block, jnp.arange(count, dtype=jnp.int32))
    return jnp.transpose(stacked, (1, 0, 2)).reshape(TOKENS, D)
```

```python
import functools

import jax
import jax.numpy as jnp
import numpy as np
from jax import lax
from jax.experimental import pallas as pl
from jax.experimental.pallas import tpu as pltpu
from jax.sharding import PartitionSpec as P

MESH = pl.DeviceIdType.MESH
f32, bf16 = jnp.float32, jnp.bfloat16

NODES = 12
ROWS = 16


def node_places(block):
    j = np.arange(NODES)
    return (block - 1) / 2 * (1 - np.cos(np.pi * (2 * j + 1) / (2 * NODES)))


def cardinals(points, nodes):
    out = np.ones((NODES,) + points.shape)
    for j in range(NODES):
        for i in range(NODES):
            if i != j:
                out[j] *= (points - nodes[i]) / (nodes[j] - nodes[i])
    return out


def constant_tables(block):
    nodes = node_places(block)
    t = np.arange(block)
    lag = t[:, None] - t[None, :]
    toeplitz = np.where(lag >= 0, cardinals(np.abs(lag).astype(float), nodes), 0.0)
    toeplitz = toeplitz.transpose(1, 0, 2).reshape(block, NODES * block)
    basis = np.zeros((block, ROWS))
    basis[:, :NODES] = cardinals(t.astype(float), nodes).T
    moment = basis[::-1].T
    return toeplitz, moment, basis


def kernel(
    n_seq, n_chan, cores, feat_hbm, taps, decay, residue, skip, toeplitz, moment, basis, out,
    feat, prod, gate, y, gx, modes, starts, border, b_send, b_recv,
    g_all, m_send, m_recv, z_send, z_recv, h_send, h_recv,
    copy_sem, b_ss, b_rs, g_ss, g_rs, m_ss, m_rs, h_ss, h_rs, z_ss, z_rs,
):
    streams, block, width = feat.shape
    n_taps = taps.shape[1]
    members = n_chan * cores
    planes = n_seq // cores
    own_width = width // members
    chan_width = width // n_chan
    fold = b_send.shape[1]
    folds = width // fold
    nodes = [float(v) for v in node_places(block)]

    seq, chan = lax.axis_index("seq"), lax.axis_index("chan")
    plane, core = seq // cores, lax.rem(seq, cores)
    me = core * n_chan + chan

    def member(i):
        return (plane * cores + i // n_chan, lax.rem(i, n_chan))

    def columns(i):
        start = lax.rem(i, n_chan) * chan_width + (i // n_chan) * own_width
        return pl.ds(pl.multiple_of(start, own_width), own_width)

    def other(i):
        return lax.rem(me + i, members)

    for m in range(streams):
        pltpu.make_async_copy(feat_hbm.at[m], feat.at[m], copy_sem.at[m]).start()

    barrier = pltpu.get_barrier_semaphore()

    @pl.loop(1, members)
    def _(i):
        pl.semaphore_signal(barrier, inc=1, device_id=member(other(i)), device_id_type=MESH)

    @pl.loop(1, planes)
    def _(i):
        there = lax.rem(plane + i, planes) * cores + core
        pl.semaphore_signal(barrier, inc=1, device_id=(there, chan), device_id_type=MESH)

    enters = jnp.logical_and(me == 0, plane > 0)
    leaves = jnp.logical_and(me == members - 1, plane < planes - 1)

    @pl.when(enters)
    def _():
        pl.semaphore_signal(
            barrier, inc=1, device_id=(plane * cores - 1, n_chan - 1), device_id_type=MESH)

    @pl.when(leaves)
    def _():
        pl.semaphore_signal(
            barrier, inc=1, device_id=((plane + 1) * cores, 0), device_id_type=MESH)

    own = pl.ds(pl.multiple_of(core * own_width, own_width), own_width)
    rate = decay[:, own]
    scaled = residue[:, own] * jnp.sqrt(1.0 - jnp.exp(-2.0 * rate))
    rows = []
    for j in range(NODES):
        a = jnp.exp(-rate * nodes[j])
        modes[j] = a
        rows.append(jnp.sum(scaled * a, axis=0, keepdims=True))
    gain = skip[:, own]
    gain_top = gain.astype(bf16).astype(f32)
    rows += [gain_top, gain - gain_top]
    rows += [jnp.zeros_like(gain)] * (ROWS - len(rows))
    g_all[me] = jnp.concatenate(rows, axis=0).astype(bf16)

    for m in range(streams):
        pltpu.make_async_copy(feat_hbm.at[m], feat.at[m], copy_sem.at[m]).wait()
    rows = []
    for m in range(streams):
        last = feat[m, block - 16:, :].astype(f32)
        for k in range(n_taps - 1):
            row = 16 - (n_taps - 1) + k
            rows += [last[row:row + 1, f * fold:(f + 1) * fold] for f in range(folds)]
    rows += [jnp.zeros_like(rows[0])] * (b_send.shape[0] - len(rows))
    b_send[...] = jnp.concatenate(rows, axis=0).astype(bf16)

    extra = jnp.where(enters, 1, 0) + jnp.where(leaves, 1, 0)
    pl.semaphore_wait(barrier, members - 1 + planes - 1 + extra)

    position = seq * n_chan + chan
    total = n_seq * n_chan
    after = lax.rem(position + 1, total)
    b_copy = pltpu.make_async_remote_copy(
        src_ref=b_send, dst_ref=b_recv, send_sem=b_ss, recv_sem=b_rs,
        device_id=(after // n_chan, lax.rem(after, n_chan)), device_id_type=MESH)

    @pl.when(position < total - 1)
    def _():
        b_copy.start()

    def g_copy(i, slot):
        return pltpu.make_async_remote_copy(
            src_ref=g_all.at[slot], dst_ref=g_all.at[slot], send_sem=g_ss.at[i],
            recv_sem=g_rs.at[slot], device_id=member(i), device_id_type=MESH)

    def m_copy(i, slot):
        return pltpu.make_async_remote_copy(
            src_ref=m_send.at[i], dst_ref=m_recv.at[slot], send_sem=m_ss.at[i],
            recv_sem=m_rs.at[slot], device_id=member(i), device_id_type=MESH)

    def h_copy(i, slot):
        return pltpu.make_async_remote_copy(
            src_ref=h_send.at[i], dst_ref=h_recv.at[slot], send_sem=h_ss.at[i],
            recv_sem=h_rs.at[slot], device_id=member(i), device_id_type=MESH)

    def z_copy(i, slot):
        return pltpu.make_async_remote_copy(
            src_ref=z_send, dst_ref=z_recv.at[slot], send_sem=z_ss.at[i],
            recv_sem=z_rs.at[slot], device_id=(i * cores + core, chan), device_id_type=MESH)

    @pl.loop(1, members)
    def _(i):
        g_copy(other(i), me).start()

    @pl.when(position > 0)
    def _():
        b_copy.wait_recv()
        got = b_recv[...].astype(f32)
        for m in range(streams):
            for k in range(n_taps - 1):
                for f in range(folds):
                    row = (m * (n_taps - 1) + k) * folds + f
                    border[m * (n_taps - 1) + k:m * (n_taps - 1) + k + 1,
                           f * fold:(f + 1) * fold] = got[row:row + 1]

    @pl.when(position == 0)
    def _():
        border[...] = jnp.zeros_like(border)

    top_row = lax.broadcasted_iota(jnp.int32, (8, own_width), 0)

    def short_filter(m, cols):
        x = feat[m, :, cols].astype(f32)
        total = taps[m, 0:1, cols] * x
        for j in range(1, n_taps):
            moved = pltpu.roll(x, j, 0)
            top = moved[:8]
            for k in range(j):
                place = m * (n_taps - 1) + n_taps - 1 - j + k
                top = jnp.where(top_row == k, border[place:place + 1, cols], top)
            moved = jnp.concatenate([top, moved[8:]], axis=0)
            total = total + taps[m, j:j + 1, cols] * moved
        return total.astype(bf16)

    @pl.loop(1, members + 1)
    def _(i):
        to = other(i)
        cols = columns(to)
        p = (short_filter(1, cols).astype(f32) * short_filter(2, cols).astype(f32)).astype(bf16)
        prod[:, cols] = p
        found = jnp.dot(moment[...], p, preferred_element_type=f32).astype(bf16)

        @pl.when(i < members)
        def _():
            m_send[to] = found
            m_copy(to, me).start()

        @pl.when(i == members)
        def _():
            m_recv[me] = found

    @pl.loop(0, members)
    def _(i):
        cols = columns(i)
        gate[:, cols] = short_filter(0, cols)

    block_decay = jnp.exp(-rate * block)

    @pl.loop(1, members)
    def _(i):
        m_copy(other(i), other(i)).wait_recv()

    def gather_block(b, state):
        starts[b] = state
        found = m_recv[b].astype(f32)
        state = block_decay * state
        for j in range(NODES):
            state = state + modes[j] * found[j:j + 1]
        return state

    final = lax.fori_loop(0, members, gather_block, jnp.zeros_like(rate))
    z_send[...] = final.astype(bf16)

    @pl.loop(plane + 1, planes)
    def _(i):
        z_copy(i, plane).start()

    @pl.loop(1, members)
    def _(i):
        g_copy(other(i), other(i)).wait_recv()

    @pl.loop(0, members)
    def _(i):
        cols = columns(i)
        p = prod[:, cols]
        g = g_all[i].astype(f32)
        for j in range(NODES):
            gx[j * block:(j + 1) * block, :] = (
                jnp.broadcast_to(g[j:j + 1], p.shape).astype(bf16) * p)
        inner = jnp.dot(toeplitz[...], gx[...], preferred_element_type=f32)
        both = g[NODES:NODES + 1] + g[NODES + 1:NODES + 2]
        y[:, cols] = inner + both * p.astype(f32)

    plane_decay = jnp.exp(-rate * (block * members))

    def gather_plane(i, state):
        z_copy(i, i).wait_recv()
        return plane_decay * state + z_recv[i].astype(f32)

    entering = lax.fori_loop(0, plane, gather_plane, jnp.zeros_like(rate))
    reading = scaled * jnp.exp(-rate)

    def respond(b, state):
        weighted = reading * (starts[b] + state)
        rows = [jnp.sum(modes[j] * weighted, axis=0, keepdims=True) for j in range(NODES)]
        rows += [jnp.zeros_like(rows[0])] * (ROWS - NODES)
        answer = jnp.concatenate(rows, axis=0).astype(bf16)

        @pl.when(b != me)
        def _():
            h_send[b] = answer
            h_copy(b, me).start()

        @pl.when(b == me)
        def _():
            h_recv[me] = answer

        return block_decay * state

    lax.fori_loop(0, members, respond, entering)

    @pl.loop(0, members)
    def _(i):
        at = other(i)
        cols = columns(at)

        @pl.when(i > 0)
        def _():
            h_copy(at, at).wait_recv()

        carried = jnp.dot(basis[...], h_recv[at], preferred_element_type=f32)
        conv = (y[:, cols] + carried).astype(bf16)
        out[:, cols] = (gate[:, cols].astype(f32) * conv.astype(f32)).astype(bf16)

    @pl.when(position < total - 1)
    def _():
        b_copy.wait_send()

    @pl.loop(1, members)
    def _(i):
        g_copy(other(i), me).wait_send()
        m_copy(other(i), me).wait_send()
        h_copy(other(i), me).wait_send()

    @pl.loop(plane + 1, planes)
    def _(i):
        z_copy(i, plane).wait_send()


def local(n_seq, n_chan, features, short_weight, decay_rate, residue, skip_gain):
    streams, block, width = features.shape
    modes = decay_rate.shape[0]
    cores = 2 if n_seq % 2 == 0 else 1
    members = n_chan * cores
    planes = n_seq // cores
    own_width = width // members
    halo = streams * (short_weight.shape[1] - 1)
    fold = width // 4
    halo_rows = -(-halo * 4 // 16) * 16
    toeplitz, moment, basis = constant_tables(block)
    vmem = pl.BlockSpec(memory_space=pltpu.VMEM)
    dma = pltpu.SemaphoreType.DMA
    small = pltpu.VMEM((members, ROWS, own_width), bf16)
    return pl.pallas_call(
        functools.partial(kernel, n_seq, n_chan, cores),
        out_shape=jax.ShapeDtypeStruct((block, width), bf16),
        in_specs=[pl.BlockSpec(memory_space=pl.ANY)] + [vmem] * 7,
        out_specs=vmem,
        scratch_shapes=[
            pltpu.VMEM((streams, block, width), bf16),
            pltpu.VMEM((block, width), bf16),
            pltpu.VMEM((block, width), bf16),
            pltpu.VMEM((block, width), f32),
            pltpu.VMEM((NODES * block, own_width), bf16),
            pltpu.VMEM((NODES, modes, own_width), f32),
            pltpu.VMEM((members, modes, own_width), f32),
            pltpu.VMEM((-(-halo // 8) * 8, width), f32),
            pltpu.VMEM((halo_rows, fold), bf16),
            pltpu.VMEM((halo_rows, fold), bf16),
            small, small, small,
            pltpu.VMEM((modes, own_width), bf16),
            pltpu.VMEM((planes, modes, own_width), bf16),
            small, small,
            dma((streams,)), dma, dma,
            dma((members,)), dma((members,)), dma((members,)), dma((members,)),
            dma((members,)), dma((members,)), dma((planes,)), dma((planes,)),
        ],
        compiler_params=pltpu.CompilerParams(
            collective_id=0, has_side_effects=True, vmem_limit_bytes=40 * 2**20),
        cost_estimate=pl.CostEstimate(
            flops=2 * block * NODES * block * width,
            bytes_accessed=8 * block * width, transcendentals=0),
    )(
        features, short_weight, decay_rate, residue, skip_gain.reshape(1, -1),
        jnp.asarray(toeplitz, bf16), jnp.asarray(moment, bf16), jnp.asarray(basis, bf16),
    )


def solution(mesh):
    return jax.shard_map(
        functools.partial(local, mesh.shape["seq"], mesh.shape["chan"]),
        mesh=mesh,
        in_specs=(P(None, ("seq", "chan"), None), P(), P(None, "chan"), P(None, "chan"), P("chan")),
        out_specs=P(("seq", "chan"), None),
        check_vma=False,
    )
```

```python
import functools

import jax
import jax.numpy as jnp
import numpy as np
from jax import lax
from jax.experimental import pallas as pl
from jax.experimental.pallas import tpu as pltpu
from jax.sharding import PartitionSpec as P

MESH = pl.DeviceIdType.MESH
f32, bf16 = jnp.float32, jnp.bfloat16

NODES = 12
ROWS = 16


def node_places(block):
    j = np.arange(NODES)
    return (block - 1) / 2 * (1 - np.cos(np.pi * (2 * j + 1) / (2 * NODES)))


def cardinals(points, nodes):
    out = np.ones((NODES,) + points.shape)
    for j in range(NODES):
        for i in range(NODES):
            if i != j:
                out[j] *= (points - nodes[i]) / (nodes[j] - nodes[i])
    return out


def constant_tables(block):
    nodes = node_places(block)
    t = np.arange(block)
    lag = t[:, None] - t[None, :]
    toeplitz = np.where(lag >= 0, cardinals(np.abs(lag).astype(float), nodes), 0.0)
    toeplitz = toeplitz.transpose(1, 0, 2).reshape(block, NODES * block)
    basis = np.zeros((block, ROWS))
    basis[:, :NODES] = cardinals(t.astype(float), nodes).T
    moment = basis[::-1].T
    return toeplitz, moment, basis


def kernel(
    n_seq, n_chan, cores, feat_hbm, taps_hbm, decay_hbm, residue_hbm, skip_hbm, toeplitz_hbm,
    moment_hbm, basis_hbm, out,
    feat, tail, taps, decay, residue, skip, toeplitz, moment, basis, prod, gate, y, gx, modes, starts, border, b_send, b_recv,
    g_all, m_send, m_recv, z_send, z_recv, h_send, h_recv,
    load_sem, store_sem, b_ss, b_rs, g_ss, g_rs, m_ss, m_rs, h_ss, h_rs, z_ss, z_rs,
):
    streams, block, width = feat.shape
    n_taps = taps.shape[1]
    members = n_chan * cores
    planes = n_seq // cores
    own_width = width // members
    chan_width = width // n_chan
    fold = b_send.shape[1]
    folds = width // fold
    nodes = [float(v) for v in node_places(block)]

    seq, chan = lax.axis_index("seq"), lax.axis_index("chan")
    plane, core = seq // cores, lax.rem(seq, cores)
    me = core * n_chan + chan

    def member(i):
        return (plane * cores + i // n_chan, lax.rem(i, n_chan))

    def columns(i):
        start = lax.rem(i, n_chan) * chan_width + (i // n_chan) * own_width
        return pl.ds(pl.multiple_of(start, own_width), own_width)

    def other(i):
        return lax.rem(me + i, members)

    own = pl.ds(pl.multiple_of(core * own_width, own_width), own_width)
    places = [
        (feat_hbm.at[:, pl.ds(block - 16, 16), :], tail),
        (decay_hbm.at[:, own], decay), (residue_hbm.at[:, own], residue),
        (skip_hbm.at[:, own], skip), (taps_hbm, taps),
        (feat_hbm.at[1], feat.at[1]), (feat_hbm.at[2], feat.at[2]),
        (moment_hbm, moment), (feat_hbm.at[0], feat.at[0]),
        (toeplitz_hbm, toeplitz), (basis_hbm, basis),
    ]
    loads = [pltpu.make_async_copy(a, b, load_sem.at[k]) for k, (a, b) in enumerate(places)]
    for load in loads:
        load.start()

    barrier = pltpu.get_barrier_semaphore()

    @pl.loop(1, members)
    def _(i):
        pl.semaphore_signal(barrier, inc=1, device_id=member(other(i)), device_id_type=MESH)

    @pl.loop(1, planes)
    def _(i):
        there = lax.rem(plane + i, planes) * cores + core
        pl.semaphore_signal(barrier, inc=1, device_id=(there, chan), device_id_type=MESH)

    enters = jnp.logical_and(me == 0, plane > 0)
    leaves = jnp.logical_and(me == members - 1, plane < planes - 1)

    @pl.when(enters)
    def _():
        pl.semaphore_signal(
            barrier, inc=1, device_id=(plane * cores - 1, n_chan - 1), device_id_type=MESH)

    @pl.when(leaves)
    def _():
        pl.semaphore_signal(
            barrier, inc=1, device_id=((plane + 1) * cores, 0), device_id_type=MESH)

    loads[0].wait()
    rows = []
    for m in range(streams):
        last = tail[m].astype(f32)
        for k in range(n_taps - 1):
            row = 16 - (n_taps - 1) + k
            rows += [last[row:row + 1, f * fold:(f + 1) * fold] for f in range(folds)]
    rows += [jnp.zeros_like(rows[0])] * (b_send.shape[0] - len(rows))
    b_send[...] = jnp.concatenate(rows, axis=0).astype(bf16)

    extra = jnp.where(enters, 1, 0) + jnp.where(leaves, 1, 0)
    pl.semaphore_wait(barrier, members - 1 + planes - 1 + extra)

    position = seq * n_chan + chan
    total = n_seq * n_chan
    after = lax.rem(position + 1, total)
    b_copy = pltpu.make_async_remote_copy(
        src_ref=b_send, dst_ref=b_recv, send_sem=b_ss, recv_sem=b_rs,
        device_id=(after // n_chan, lax.rem(after, n_chan)), device_id_type=MESH)

    @pl.when(position < total - 1)
    def _():
        b_copy.start()

    def g_copy(i, slot):
        return pltpu.make_async_remote_copy(
            src_ref=g_all.at[slot], dst_ref=g_all.at[slot], send_sem=g_ss.at[i],
            recv_sem=g_rs.at[slot], device_id=member(i), device_id_type=MESH)

    def m_copy(i, slot):
        return pltpu.make_async_remote_copy(
            src_ref=m_send.at[i], dst_ref=m_recv.at[slot], send_sem=m_ss.at[i],
            recv_sem=m_rs.at[slot], device_id=member(i), device_id_type=MESH)

    def h_copy(i, slot):
        return pltpu.make_async_remote_copy(
            src_ref=h_send.at[i], dst_ref=h_recv.at[slot], send_sem=h_ss.at[i],
            recv_sem=h_rs.at[slot], device_id=member(i), device_id_type=MESH)

    def z_copy(i, slot):
        return pltpu.make_async_remote_copy(
            src_ref=z_send, dst_ref=z_recv.at[slot], send_sem=z_ss.at[i],
            recv_sem=z_rs.at[slot], device_id=(i * cores + core, chan), device_id_type=MESH)

    for load in loads[1:4]:
        load.wait()
    rate = decay[...]
    scaled = residue[...] * jnp.sqrt(1.0 - jnp.exp(-2.0 * rate))
    rows = []
    for j in range(NODES):
        a = jnp.exp(-rate * nodes[j])
        modes[j] = a
        rows.append(jnp.sum(scaled * a, axis=0, keepdims=True))
    gain = skip[...]
    gain_top = gain.astype(bf16).astype(f32)
    rows += [gain_top, gain - gain_top]
    rows += [jnp.zeros_like(gain)] * (ROWS - len(rows))
    g_all[me] = jnp.concatenate(rows, axis=0).astype(bf16)

    @pl.loop(1, members)
    def _(i):
        g_copy(other(i), me).start()

    top_row = lax.broadcasted_iota(jnp.int32, (8, own_width), 0)

    def short_filter(m, cols, rows, with_border):
        x = feat[m, :rows, cols].astype(f32)
        total = taps[m, 0:1, cols] * x
        for j in range(1, n_taps):
            moved = pltpu.roll(x, j, 0)
            if with_border:
                top = moved[:8]
                for k in range(j):
                    place = m * (n_taps - 1) + n_taps - 1 - j + k
                    top = jnp.where(top_row == k, border[place:place + 1, cols], top)
                moved = jnp.concatenate([top, moved[8:]], axis=0)
            total = total + taps[m, j:j + 1, cols] * moved
        return total.astype(bf16)

    def product(cols, rows, with_border):
        left = short_filter(1, cols, rows, with_border).astype(f32)
        return (left * short_filter(2, cols, rows, with_border).astype(f32)).astype(bf16)

    for load in loads[4:7]:
        load.wait()

    @pl.loop(0, members)
    def _(i):
        cols = columns(i)
        prod[:, cols] = product(cols, block, False)

    @pl.when(position > 0)
    def _():
        b_copy.wait_recv()
        got = b_recv[...].astype(f32)
        for m in range(streams):
            for k in range(n_taps - 1):
                for f in range(folds):
                    row = (m * (n_taps - 1) + k) * folds + f
                    border[m * (n_taps - 1) + k:m * (n_taps - 1) + k + 1,
                           f * fold:(f + 1) * fold] = got[row:row + 1]

    @pl.when(position == 0)
    def _():
        border[...] = jnp.zeros_like(border)

    loads[7].wait()

    @pl.loop(1, members + 1)
    def _(i):
        to = other(i)
        cols = columns(to)
        prod[:16, cols] = product(cols, 16, True)
        found = jnp.dot(moment[...], prod[:, cols], preferred_element_type=f32).astype(bf16)

        @pl.when(i < members)
        def _():
            m_send[to] = found
            m_copy(to, me).start()

        @pl.when(i == members)
        def _():
            m_recv[me] = found

    loads[8].wait()

    @pl.loop(0, members)
    def _(i):
        cols = columns(i)
        gate[:, cols] = short_filter(0, cols, block, True)

    block_decay = jnp.exp(-rate * block)

    @pl.loop(1, members)
    def _(i):
        m_copy(other(i), other(i)).wait_recv()

    def gather_block(b, state):
        starts[b] = state
        found = m_recv[b].astype(f32)
        state = block_decay * state
        for j in range(NODES):
            state = state + modes[j] * found[j:j + 1]
        return state

    final = lax.fori_loop(0, members, gather_block, jnp.zeros_like(rate))
    z_send[...] = final.astype(bf16)

    @pl.loop(plane + 1, planes)
    def _(i):
        z_copy(i, plane).start()

    @pl.loop(1, members)
    def _(i):
        g_copy(other(i), other(i)).wait_recv()

    loads[9].wait()

    def own_part(i):
        cols = columns(i)
        p = prod[:, cols]
        g = g_all[i].astype(f32)
        for j in range(NODES):
            gx[j * block:(j + 1) * block, :] = (
                jnp.broadcast_to(g[j:j + 1], p.shape).astype(bf16) * p)
        inner = jnp.dot(toeplitz[...], gx[...], preferred_element_type=f32)
        both = g[NODES:NODES + 1] + g[NODES + 1:NODES + 2]
        y[:, cols] = inner + both * p.astype(f32)

    early = members // 2

    @pl.loop(0, early)
    def _(i):
        own_part(i)

    plane_decay = jnp.exp(-rate * (block * members))

    def gather_plane(i, state):
        z_copy(i, i).wait_recv()
        return plane_decay * state + z_recv[i].astype(f32)

    entering = lax.fori_loop(0, plane, gather_plane, jnp.zeros_like(rate))
    reading = scaled * jnp.exp(-rate)

    def respond(b, state):
        weighted = reading * (starts[b] + state)
        rows = [jnp.sum(modes[j] * weighted, axis=0, keepdims=True) for j in range(NODES)]
        rows += [jnp.zeros_like(rows[0])] * (ROWS - NODES)
        answer = jnp.concatenate(rows, axis=0).astype(bf16)

        @pl.when(b != me)
        def _():
            h_send[b] = answer
            h_copy(b, me).start()

        @pl.when(b == me)
        def _():
            h_recv[me] = answer

        return block_decay * state

    lax.fori_loop(0, members, respond, entering)

    @pl.loop(early, members)
    def _(i):
        own_part(i)

    loads[10].wait()

    def store(i):
        return pltpu.make_async_copy(
            gate.at[:, columns(i)], out.at[:, columns(i)], store_sem.at[i])

    @pl.loop(0, members)
    def _(i):
        at = other(i)
        cols = columns(at)

        @pl.when(i > 0)
        def _():
            h_copy(at, at).wait_recv()

        carried = jnp.dot(basis[...], h_recv[at], preferred_element_type=f32)
        conv = (y[:, cols] + carried).astype(bf16)
        gate[:, cols] = (gate[:, cols].astype(f32) * conv.astype(f32)).astype(bf16)
        store(at).start()

    @pl.when(position < total - 1)
    def _():
        b_copy.wait_send()

    @pl.loop(1, members)
    def _(i):
        g_copy(other(i), me).wait_send()
        m_copy(other(i), me).wait_send()
        h_copy(other(i), me).wait_send()

    @pl.loop(plane + 1, planes)
    def _(i):
        z_copy(i, plane).wait_send()

    @pl.loop(0, members)
    def _(i):
        store(i).wait()


def local(n_seq, n_chan, features, short_weight, decay_rate, residue, skip_gain):
    streams, block, width = features.shape
    modes = decay_rate.shape[0]
    cores = 2 if n_seq % 2 == 0 else 1
    members = n_chan * cores
    planes = n_seq // cores
    own_width = width // members
    halo = streams * (short_weight.shape[1] - 1)
    fold = width // 4
    halo_rows = -(-halo * 4 // 16) * 16
    toeplitz, moment, basis = constant_tables(block)
    anywhere = pl.BlockSpec(memory_space=pl.ANY)
    dma = pltpu.SemaphoreType.DMA
    small = pltpu.VMEM((members, ROWS, own_width), bf16)
    return pl.pallas_call(
        functools.partial(kernel, n_seq, n_chan, cores),
        out_shape=jax.ShapeDtypeStruct((block, width), bf16),
        in_specs=[anywhere] * 8,
        out_specs=anywhere,
        scratch_shapes=[
            pltpu.VMEM((streams, block, width), bf16),
            pltpu.VMEM((streams, 16, width), bf16),
            pltpu.VMEM(short_weight.shape, f32),
            pltpu.VMEM((modes, own_width), f32),
            pltpu.VMEM((modes, own_width), f32),
            pltpu.VMEM((1, own_width), f32),
            pltpu.VMEM(toeplitz.shape, bf16),
            pltpu.VMEM(moment.shape, bf16),
            pltpu.VMEM(basis.shape, bf16),
            pltpu.VMEM((block, width), bf16),
            pltpu.VMEM((block, width), bf16),
            pltpu.VMEM((block, width), f32),
            pltpu.VMEM((NODES * block, own_width), bf16),
            pltpu.VMEM((NODES, modes, own_width), f32),
            pltpu.VMEM((members, modes, own_width), f32),
            pltpu.VMEM((-(-halo // 8) * 8, width), f32),
            pltpu.VMEM((halo_rows, fold), bf16),
            pltpu.VMEM((halo_rows, fold), bf16),
            small, small, small,
            pltpu.VMEM((modes, own_width), bf16),
            pltpu.VMEM((planes, modes, own_width), bf16),
            small, small,
            dma((11,)), dma((members,)), dma, dma,
            dma((members,)), dma((members,)), dma((members,)), dma((members,)),
            dma((members,)), dma((members,)), dma((planes,)), dma((planes,)),
        ],
        compiler_params=pltpu.CompilerParams(
            collective_id=0, has_side_effects=True, vmem_limit_bytes=60 * 2**20),
        cost_estimate=pl.CostEstimate(
            flops=2 * block * NODES * block * width,
            bytes_accessed=8 * block * width, transcendentals=0),
    )(
        features, short_weight, decay_rate, residue, skip_gain.reshape(1, -1),
        jnp.asarray(toeplitz, bf16), jnp.asarray(moment, bf16), jnp.asarray(basis, bf16),
    )


def solution(mesh):
    return jax.shard_map(
        functools.partial(local, mesh.shape["seq"], mesh.shape["chan"]),
        mesh=mesh,
        in_specs=(P(None, ("seq", "chan"), None), P(), P(None, "chan"), P(None, "chan"), P("chan")),
        out_specs=P(("seq", "chan"), None),
        check_vma=False,
    )
```

```python
import functools

import jax
import jax.numpy as jnp
import numpy as np
from jax import lax
from jax.experimental import pallas as pl
from jax.experimental.pallas import tpu as pltpu
from jax.sharding import PartitionSpec as P

MESH = pl.DeviceIdType.MESH
f32, bf16 = jnp.float32, jnp.bfloat16

NODES = 12
ROWS = 16


def node_places(block):
    j = np.arange(NODES)
    return (block - 1) / 2 * (1 - np.cos(np.pi * (2 * j + 1) / (2 * NODES)))


def cardinals(points, nodes):
    out = np.ones((NODES,) + points.shape)
    for j in range(NODES):
        for i in range(NODES):
            if i != j:
                out[j] *= (points - nodes[i]) / (nodes[j] - nodes[i])
    return out


def constant_tables(block):
    nodes = node_places(block)
    t = np.arange(block)
    lag = t[:, None] - t[None, :]
    toeplitz = np.where(lag >= 0, cardinals(np.abs(lag).astype(float), nodes), 0.0)
    toeplitz = toeplitz.transpose(1, 0, 2).reshape(block, NODES * block)
    basis = np.zeros((block, ROWS))
    basis[:, :NODES] = cardinals(t.astype(float), nodes).T
    moment = basis[::-1].T
    return toeplitz, moment, basis


def kernel(
    n_seq, n_chan, cores, feat_hbm, taps_hbm, decay_hbm, residue_hbm, skip_hbm, toeplitz_hbm,
    moment_hbm, basis_hbm, out,
    feat, tail, taps, decay, residue, skip, toeplitz, moment, basis, prod, gate, y, gx, modes, starts, border, b_send, b_recv,
    g_all, m_send, m_recv, z_send, z_recv, h_send, h_recv,
    load_sem, b_ss, b_rs, g_ss, g_rs, m_ss, m_rs, h_ss, h_rs, z_ss, z_rs,
):
    streams, block, width = feat.shape
    n_taps = taps.shape[1]
    members = n_chan * cores
    planes = n_seq // cores
    own_width = width // members
    chan_width = width // n_chan
    fold = b_send.shape[1]
    folds = width // fold
    nodes = [float(v) for v in node_places(block)]

    seq, chan = lax.axis_index("seq"), lax.axis_index("chan")
    plane, core = seq // cores, lax.rem(seq, cores)
    me = core * n_chan + chan

    def member(i):
        return (plane * cores + i // n_chan, lax.rem(i, n_chan))

    def columns(i):
        start = lax.rem(i, n_chan) * chan_width + (i // n_chan) * own_width
        return pl.ds(pl.multiple_of(start, own_width), own_width)

    def other(i):
        return lax.rem(me + i, members)

    own = pl.ds(pl.multiple_of(core * own_width, own_width), own_width)
    places = [
        (feat_hbm.at[:, pl.ds(block - 16, 16), :], tail),
        (decay_hbm.at[:, own], decay), (residue_hbm.at[:, own], residue),
        (skip_hbm.at[:, own], skip), (taps_hbm, taps),
        (feat_hbm.at[1], feat.at[1]), (feat_hbm.at[2], feat.at[2]),
        (moment_hbm, moment), (feat_hbm.at[0], feat.at[0]),
        (toeplitz_hbm, toeplitz), (basis_hbm, basis),
    ]
    loads = [pltpu.make_async_copy(a, b, load_sem.at[k]) for k, (a, b) in enumerate(places)]
    for load in loads:
        load.start()

    barrier = pltpu.get_barrier_semaphore()

    @pl.loop(1, members)
    def _(i):
        pl.semaphore_signal(barrier, inc=1, device_id=member(other(i)), device_id_type=MESH)

    @pl.loop(1, planes)
    def _(i):
        there = lax.rem(plane + i, planes) * cores + core
        pl.semaphore_signal(barrier, inc=1, device_id=(there, chan), device_id_type=MESH)

    enters = jnp.logical_and(me == 0, plane > 0)
    leaves = jnp.logical_and(me == members - 1, plane < planes - 1)

    @pl.when(enters)
    def _():
        pl.semaphore_signal(
            barrier, inc=1, device_id=(plane * cores - 1, n_chan - 1), device_id_type=MESH)

    @pl.when(leaves)
    def _():
        pl.semaphore_signal(
            barrier, inc=1, device_id=((plane + 1) * cores, 0), device_id_type=MESH)

    loads[0].wait()
    rows = []
    for m in range(streams):
        last = tail[m].astype(f32)
        for k in range(n_taps - 1):
            row = 16 - (n_taps - 1) + k
            rows += [last[row:row + 1, f * fold:(f + 1) * fold] for f in range(folds)]
    rows += [jnp.zeros_like(rows[0])] * (b_send.shape[0] - len(rows))
    b_send[...] = jnp.concatenate(rows, axis=0).astype(bf16)

    extra = jnp.where(enters, 1, 0) + jnp.where(leaves, 1, 0)
    pl.semaphore_wait(barrier, members - 1 + planes - 1 + extra)

    position = seq * n_chan + chan
    total = n_seq * n_chan
    after = lax.rem(position + 1, total)
    b_copy = pltpu.make_async_remote_copy(
        src_ref=b_send, dst_ref=b_recv, send_sem=b_ss, recv_sem=b_rs,
        device_id=(after // n_chan, lax.rem(after, n_chan)), device_id_type=MESH)

    @pl.when(position < total - 1)
    def _():
        b_copy.start()

    def g_copy(i, slot):
        return pltpu.make_async_remote_copy(
            src_ref=g_all.at[slot], dst_ref=g_all.at[slot], send_sem=g_ss.at[i],
            recv_sem=g_rs.at[slot], device_id=member(i), device_id_type=MESH)

    def m_copy(i, slot):
        return pltpu.make_async_remote_copy(
            src_ref=m_send.at[i], dst_ref=m_recv.at[slot], send_sem=m_ss.at[i],
            recv_sem=m_rs.at[slot], device_id=member(i), device_id_type=MESH)

    def h_copy(i, slot):
        return pltpu.make_async_remote_copy(
            src_ref=h_send.at[i], dst_ref=h_recv.at[slot], send_sem=h_ss.at[i],
            recv_sem=h_rs.at[slot], device_id=member(i), device_id_type=MESH)

    def z_copy(i, slot):
        return pltpu.make_async_remote_copy(
            src_ref=z_send, dst_ref=z_recv.at[slot], send_sem=z_ss.at[i],
            recv_sem=z_rs.at[slot], device_id=(i * cores + core, chan), device_id_type=MESH)

    for load in loads[1:4]:
        load.wait()
    rate = decay[...]
    scaled = residue[...] * jnp.sqrt(1.0 - jnp.exp(-2.0 * rate))
    rows = []
    for j in range(NODES):
        a = jnp.exp(-rate * nodes[j])
        modes[j] = a
        rows.append(jnp.sum(scaled * a, axis=0, keepdims=True))
    gain = skip[...]
    gain_top = gain.astype(bf16).astype(f32)
    rows += [gain_top, gain - gain_top]
    rows += [jnp.zeros_like(gain)] * (ROWS - len(rows))
    g_all[me] = jnp.concatenate(rows, axis=0).astype(bf16)

    @pl.loop(1, members)
    def _(i):
        g_copy(other(i), me).start()

    top_row = lax.broadcasted_iota(jnp.int32, (8, own_width), 0)

    def short_filter(m, cols, rows, with_border):
        x = feat[m, :rows, cols].astype(f32)
        total = taps[m, 0:1, cols] * x
        for j in range(1, n_taps):
            moved = pltpu.roll(x, j, 0)
            if with_border:
                top = moved[:8]
                for k in range(j):
                    place = m * (n_taps - 1) + n_taps - 1 - j + k
                    top = jnp.where(top_row == k, border[place:place + 1, cols], top)
                moved = jnp.concatenate([top, moved[8:]], axis=0)
            total = total + taps[m, j:j + 1, cols] * moved
        return total.astype(bf16)

    def product(cols, rows, with_border):
        left = short_filter(1, cols, rows, with_border).astype(f32)
        return (left * short_filter(2, cols, rows, with_border).astype(f32)).astype(bf16)

    for load in loads[4:7]:
        load.wait()

    @pl.loop(0, members)
    def _(i):
        cols = columns(i)
        prod[:, cols] = product(cols, block, False)

    @pl.when(position > 0)
    def _():
        b_copy.wait_recv()
        got = b_recv[...].astype(f32)
        for m in range(streams):
            for k in range(n_taps - 1):
                for f in range(folds):
                    row = (m * (n_taps - 1) + k) * folds + f
                    border[m * (n_taps - 1) + k:m * (n_taps - 1) + k + 1,
                           f * fold:(f + 1) * fold] = got[row:row + 1]

    @pl.when(position == 0)
    def _():
        border[...] = jnp.zeros_like(border)

    loads[7].wait()

    @pl.loop(1, members + 1)
    def _(i):
        to = other(i)
        cols = columns(to)
        prod[:16, cols] = product(cols, 16, True)
        found = jnp.dot(moment[...], prod[:, cols], preferred_element_type=f32).astype(bf16)

        @pl.when(i < members)
        def _():
            m_send[to] = found
            m_copy(to, me).start()

        @pl.when(i == members)
        def _():
            m_recv[me] = found

    loads[8].wait()

    @pl.loop(0, members)
    def _(i):
        cols = columns(i)
        gate[:, cols] = short_filter(0, cols, block, True)

    block_decay = jnp.exp(-rate * block)

    @pl.loop(1, members)
    def _(i):
        m_copy(other(i), other(i)).wait_recv()

    def gather_block(b, state):
        starts[b] = state
        found = m_recv[b].astype(f32)
        state = block_decay * state
        for j in range(NODES):
            state = state + modes[j] * found[j:j + 1]
        return state

    final = lax.fori_loop(0, members, gather_block, jnp.zeros_like(rate))
    z_send[...] = final.astype(bf16)

    @pl.loop(plane + 1, planes)
    def _(i):
        z_copy(i, plane).start()

    @pl.loop(1, members)
    def _(i):
        g_copy(other(i), other(i)).wait_recv()

    loads[9].wait()

    def own_part(i):
        cols = columns(i)
        p = prod[:, cols]
        g = g_all[i].astype(f32)
        for j in range(NODES):
            gx[j * block:(j + 1) * block, :] = (
                jnp.broadcast_to(g[j:j + 1], p.shape).astype(bf16) * p)
        inner = jnp.dot(toeplitz[...], gx[...], preferred_element_type=f32)
        both = g[NODES:NODES + 1] + g[NODES + 1:NODES + 2]
        y[:, cols] = inner + both * p.astype(f32)

    early = members // 2

    @pl.loop(0, early)
    def _(i):
        own_part(i)

    plane_decay = jnp.exp(-rate * (block * members))

    def gather_plane(i, state):
        z_copy(i, i).wait_recv()
        return plane_decay * state + z_recv[i].astype(f32)

    entering = lax.fori_loop(0, plane, gather_plane, jnp.zeros_like(rate))
    reading = scaled * jnp.exp(-rate)

    def respond(b, state):
        weighted = reading * (starts[b] + state)
        rows = [jnp.sum(modes[j] * weighted, axis=0, keepdims=True) for j in range(NODES)]
        rows += [jnp.zeros_like(rows[0])] * (ROWS - NODES)
        answer = jnp.concatenate(rows, axis=0).astype(bf16)

        @pl.when(b != me)
        def _():
            h_send[b] = answer
            h_copy(b, me).start()

        @pl.when(b == me)
        def _():
            h_recv[me] = answer

        return block_decay * state

    lax.fori_loop(0, members, respond, entering)

    @pl.loop(early, members)
    def _(i):
        own_part(i)

    loads[10].wait()

    @pl.loop(0, members)
    def _(i):
        at = other(i)
        cols = columns(at)

        @pl.when(i > 0)
        def _():
            h_copy(at, at).wait_recv()

        carried = jnp.dot(basis[...], h_recv[at], preferred_element_type=f32)
        conv = (y[:, cols] + carried).astype(bf16)
        out[:, cols] = (gate[:, cols].astype(f32) * conv.astype(f32)).astype(bf16)

    @pl.when(position < total - 1)
    def _():
        b_copy.wait_send()

    @pl.loop(1, members)
    def _(i):
        g_copy(other(i), me).wait_send()
        m_copy(other(i), me).wait_send()
        h_copy(other(i), me).wait_send()

    @pl.loop(plane + 1, planes)
    def _(i):
        z_copy(i, plane).wait_send()


def local(n_seq, n_chan, features, short_weight, decay_rate, residue, skip_gain):
    streams, block, width = features.shape
    modes = decay_rate.shape[0]
    cores = 2 if n_seq % 2 == 0 else 1
    members = n_chan * cores
    planes = n_seq // cores
    own_width = width // members
    halo = streams * (short_weight.shape[1] - 1)
    fold = width // 4
    halo_rows = -(-halo * 4 // 16) * 16
    toeplitz, moment, basis = constant_tables(block)
    anywhere = pl.BlockSpec(memory_space=pl.ANY)
    dma = pltpu.SemaphoreType.DMA
    small = pltpu.VMEM((members, ROWS, own_width), bf16)
    return pl.pallas_call(
        functools.partial(kernel, n_seq, n_chan, cores),
        out_shape=pltpu.VMEM((block, width), bf16),
        in_specs=[anywhere] * 8,
        out_specs=pl.BlockSpec(memory_space=pltpu.VMEM),
        scratch_shapes=[
            pltpu.VMEM((streams, block, width), bf16),
            pltpu.VMEM((streams, 16, width), bf16),
            pltpu.VMEM(short_weight.shape, f32),
            pltpu.VMEM((modes, own_width), f32),
            pltpu.VMEM((modes, own_width), f32),
            pltpu.VMEM((1, own_width), f32),
            pltpu.VMEM(toeplitz.shape, bf16),
            pltpu.VMEM(moment.shape, bf16),
            pltpu.VMEM(basis.shape, bf16),
            pltpu.VMEM((block, width), bf16),
            pltpu.VMEM((block, width), bf16),
            pltpu.VMEM((block, width), f32),
            pltpu.VMEM((NODES * block, own_width), bf16),
            pltpu.VMEM((NODES, modes, own_width), f32),
            pltpu.VMEM((members, modes, own_width), f32),
            pltpu.VMEM((-(-halo // 8) * 8, width), f32),
            pltpu.VMEM((halo_rows, fold), bf16),
            pltpu.VMEM((halo_rows, fold), bf16),
            small, small, small,
            pltpu.VMEM((modes, own_width), bf16),
            pltpu.VMEM((planes, modes, own_width), bf16),
            small, small,
            dma((11,)), dma, dma,
            dma((members,)), dma((members,)), dma((members,)), dma((members,)),
            dma((members,)), dma((members,)), dma((planes,)), dma((planes,)),
        ],
        compiler_params=pltpu.CompilerParams(
            collective_id=0, has_side_effects=True, vmem_limit_bytes=60 * 2**20),
        cost_estimate=pl.CostEstimate(
            flops=2 * block * NODES * block * width,
            bytes_accessed=8 * block * width, transcendentals=0),
    )(
        features, short_weight, decay_rate, residue, skip_gain.reshape(1, -1),
        jnp.asarray(toeplitz, bf16), jnp.asarray(moment, bf16), jnp.asarray(basis, bf16),
    )


def solution(mesh):
    return jax.shard_map(
        functools.partial(local, mesh.shape["seq"], mesh.shape["chan"]),
        mesh=mesh,
        in_specs=(P(None, ("seq", "chan"), None), P(), P(None, "chan"), P(None, "chan"), P("chan")),
        out_specs=P(("seq", "chan"), None),
        check_vma=False,
    )
```

```python
import functools

import jax
import jax.numpy as jnp
import numpy as np
from jax import lax
from jax.experimental import pallas as pl
from jax.experimental.pallas import tpu as pltpu
from jax.sharding import PartitionSpec as P

MESH = pl.DeviceIdType.MESH
f32, bf16 = jnp.float32, jnp.bfloat16

NODES = 12
ROWS = 16
LANES = 128


def node_places(block):
    j = np.arange(NODES)
    return (block - 1) / 2 * (1 - np.cos(np.pi * (2 * j + 1) / (2 * NODES)))


def cardinals(points, nodes):
    out = np.ones((NODES,) + points.shape)
    for j in range(NODES):
        for i in range(NODES):
            if i != j:
                out[j] *= (points - nodes[i]) / (nodes[j] - nodes[i])
    return out


def constant_tables(block):
    nodes = node_places(block)
    t = np.arange(block)
    lag = t[:, None] - t[None, :]
    toeplitz = np.where(lag >= 0, cardinals(np.abs(lag).astype(float), nodes), 0.0)
    toeplitz = toeplitz.transpose(1, 0, 2).reshape(block, NODES * block)
    basis = np.zeros((block, ROWS))
    basis[:, :NODES] = cardinals(t.astype(float), nodes).T
    moment = basis[::-1].T
    return toeplitz, moment, basis


def kernel(
    n_seq, n_chan, cores, feat_hbm, taps_hbm, decay_hbm, residue_hbm, skip_hbm, toeplitz_hbm,
    moment_hbm, basis_hbm, out,
    feat, tail, taps, decay, residue, skip, toeplitz, moment, basis, prod, gate, y, gx, modes, starts, border, b_send, b_recv,
    g_all, m_send, m_recv, z_send, z_recv, h_send, h_recv,
    load_sem, b_ss, b_rs, g_ss, g_rs, m_ss, m_rs, h_ss, h_rs, z_ss, z_rs,
):
    streams, block, width = feat.shape
    n_taps = taps.shape[1]
    members = n_chan * cores
    planes = n_seq // cores
    own_width = width // members
    chan_width = width // n_chan
    fold = b_send.shape[1]
    folds = width // fold
    nodes = [float(v) for v in node_places(block)]

    seq, chan = lax.axis_index("seq"), lax.axis_index("chan")
    plane, core = seq // cores, lax.rem(seq, cores)
    me = core * n_chan + chan

    def member(i):
        return (plane * cores + i // n_chan, lax.rem(i, n_chan))

    def columns(i):
        start = lax.rem(i, n_chan) * chan_width + (i // n_chan) * own_width
        return pl.ds(pl.multiple_of(start, own_width), own_width)

    def strips(i):
        start = lax.rem(i, n_chan) * chan_width + (i // n_chan) * own_width
        for k in range(0, own_width, LANES):
            yield pl.ds(pl.multiple_of(start + k, LANES), LANES)

    def other(i):
        return lax.rem(me + i, members)

    own = pl.ds(pl.multiple_of(core * own_width, own_width), own_width)
    places = [
        (feat_hbm.at[:, pl.ds(block - 16, 16), :], tail),
        (decay_hbm.at[:, own], decay), (residue_hbm.at[:, own], residue),
        (skip_hbm.at[:, own], skip), (taps_hbm, taps),
        (feat_hbm.at[1], feat.at[1]), (feat_hbm.at[2], feat.at[2]),
        (moment_hbm, moment), (feat_hbm.at[0], feat.at[0]),
        (toeplitz_hbm, toeplitz), (basis_hbm, basis),
    ]
    loads = [pltpu.make_async_copy(a, b, load_sem.at[k]) for k, (a, b) in enumerate(places)]
    for load in loads:
        load.start()

    barrier = pltpu.get_barrier_semaphore()

    @pl.loop(1, members)
    def _(i):
        pl.semaphore_signal(barrier, inc=1, device_id=member(other(i)), device_id_type=MESH)

    @pl.loop(1, planes)
    def _(i):
        there = lax.rem(plane + i, planes) * cores + core
        pl.semaphore_signal(barrier, inc=1, device_id=(there, chan), device_id_type=MESH)

    enters = jnp.logical_and(me == 0, plane > 0)
    leaves = jnp.logical_and(me == members - 1, plane < planes - 1)

    @pl.when(enters)
    def _():
        pl.semaphore_signal(
            barrier, inc=1, device_id=(plane * cores - 1, n_chan - 1), device_id_type=MESH)

    @pl.when(leaves)
    def _():
        pl.semaphore_signal(
            barrier, inc=1, device_id=((plane + 1) * cores, 0), device_id_type=MESH)

    loads[0].wait()
    rows = []
    for m in range(streams):
        last = tail[m].astype(f32)
        for k in range(n_taps - 1):
            row = 16 - (n_taps - 1) + k
            rows += [last[row:row + 1, f * fold:(f + 1) * fold] for f in range(folds)]
    rows += [jnp.zeros_like(rows[0])] * (b_send.shape[0] - len(rows))
    b_send[...] = jnp.concatenate(rows, axis=0).astype(bf16)

    extra = jnp.where(enters, 1, 0) + jnp.where(leaves, 1, 0)
    pl.semaphore_wait(barrier, members - 1 + planes - 1 + extra)

    position = seq * n_chan + chan
    total = n_seq * n_chan
    after = lax.rem(position + 1, total)
    b_copy = pltpu.make_async_remote_copy(
        src_ref=b_send, dst_ref=b_recv, send_sem=b_ss, recv_sem=b_rs,
        device_id=(after // n_chan, lax.rem(after, n_chan)), device_id_type=MESH)

    @pl.when(position < total - 1)
    def _():
        b_copy.start()

    def g_copy(i, slot):
        return pltpu.make_async_remote_copy(
            src_ref=g_all.at[slot], dst_ref=g_all.at[slot], send_sem=g_ss.at[i],
            recv_sem=g_rs.at[slot], device_id=member(i), device_id_type=MESH)

    def m_copy(i, slot):
        return pltpu.make_async_remote_copy(
            src_ref=m_send.at[i], dst_ref=m_recv.at[slot], send_sem=m_ss.at[i],
            recv_sem=m_rs.at[slot], device_id=member(i), device_id_type=MESH)

    def h_copy(i, slot):
        return pltpu.make_async_remote_copy(
            src_ref=h_send.at[i], dst_ref=h_recv.at[slot], send_sem=h_ss.at[i],
            recv_sem=h_rs.at[slot], device_id=member(i), device_id_type=MESH)

    def z_copy(i, slot):
        return pltpu.make_async_remote_copy(
            src_ref=z_send, dst_ref=z_recv.at[slot], send_sem=z_ss.at[i],
            recv_sem=z_rs.at[slot], device_id=(i * cores + core, chan), device_id_type=MESH)

    for load in loads[1:4]:
        load.wait()
    rate = decay[...]
    scaled = residue[...] * jnp.sqrt(1.0 - jnp.exp(-2.0 * rate))
    rows = []
    for j in range(NODES):
        a = jnp.exp(-rate * nodes[j])
        modes[j] = a
        rows.append(jnp.sum(scaled * a, axis=0, keepdims=True))
    gain = skip[...]
    gain_top = gain.astype(bf16).astype(f32)
    rows += [gain_top, gain - gain_top]
    rows += [jnp.zeros_like(gain)] * (ROWS - len(rows))
    g_all[me] = jnp.concatenate(rows, axis=0).astype(bf16)

    @pl.loop(1, members)
    def _(i):
        g_copy(other(i), me).start()

    top_row = lax.broadcasted_iota(jnp.int32, (8, LANES), 0)

    def short_filter(m, cols, rows, with_border):
        x = feat[m, :rows, cols].astype(f32)
        total = taps[m, 0:1, cols] * x
        for j in range(1, n_taps):
            moved = pltpu.roll(x, j, 0)
            if with_border:
                top = moved[:8]
                for k in range(j):
                    place = m * (n_taps - 1) + n_taps - 1 - j + k
                    top = jnp.where(top_row == k, border[place:place + 1, cols], top)
                moved = jnp.concatenate([top, moved[8:]], axis=0)
            total = total + taps[m, j:j + 1, cols] * moved
        return total.astype(bf16)

    def product(cols, rows, with_border):
        left = short_filter(1, cols, rows, with_border).astype(f32)
        return (left * short_filter(2, cols, rows, with_border).astype(f32)).astype(bf16)

    for load in loads[4:7]:
        load.wait()

    @pl.loop(0, members)
    def _(i):
        for cols in strips(i):
            prod[:, cols] = product(cols, block, False)

    @pl.when(position > 0)
    def _():
        b_copy.wait_recv()
        got = b_recv[...].astype(f32)
        for m in range(streams):
            for k in range(n_taps - 1):
                for f in range(folds):
                    row = (m * (n_taps - 1) + k) * folds + f
                    border[m * (n_taps - 1) + k:m * (n_taps - 1) + k + 1,
                           f * fold:(f + 1) * fold] = got[row:row + 1]

    @pl.when(position == 0)
    def _():
        border[...] = jnp.zeros_like(border)

    loads[7].wait()

    @pl.loop(1, members + 1)
    def _(i):
        to = other(i)
        for cols in strips(to):
            prod[:16, cols] = product(cols, 16, True)
        found = jnp.dot(moment[...], prod[:, columns(to)], preferred_element_type=f32).astype(bf16)

        @pl.when(i < members)
        def _():
            m_send[to] = found
            m_copy(to, me).start()

        @pl.when(i == members)
        def _():
            m_recv[me] = found

    loads[8].wait()

    @pl.loop(0, members)
    def _(i):
        for cols in strips(i):
            gate[:, cols] = short_filter(0, cols, block, True)

    block_decay = jnp.exp(-rate * block)

    @pl.loop(1, members)
    def _(i):
        m_copy(other(i), other(i)).wait_recv()

    def gather_block(b, state):
        starts[b] = state
        found = m_recv[b].astype(f32)
        state = block_decay * state
        for j in range(NODES):
            state = state + modes[j] * found[j:j + 1]
        return state

    final = lax.fori_loop(0, members, gather_block, jnp.zeros_like(rate))
    z_send[...] = final.astype(bf16)

    @pl.loop(plane + 1, planes)
    def _(i):
        z_copy(i, plane).start()

    @pl.loop(1, members)
    def _(i):
        g_copy(other(i), other(i)).wait_recv()

    loads[9].wait()

    def own_part(i):
        cols = columns(i)
        p = prod[:, cols]
        g = g_all[i].astype(f32)
        for j in range(NODES):
            gx[j * block:(j + 1) * block, :] = (
                jnp.broadcast_to(g[j:j + 1], p.shape).astype(bf16) * p)
        inner = jnp.dot(toeplitz[...], gx[...], preferred_element_type=f32)
        both = g[NODES:NODES + 1] + g[NODES + 1:NODES + 2]
        y[:, cols] = inner + both * p.astype(f32)

    early = members // 2

    @pl.loop(0, early)
    def _(i):
        own_part(i)

    plane_decay = jnp.exp(-rate * (block * members))

    def gather_plane(i, state):
        z_copy(i, i).wait_recv()
        return plane_decay * state + z_recv[i].astype(f32)

    entering = lax.fori_loop(0, plane, gather_plane, jnp.zeros_like(rate))
    reading = scaled * jnp.exp(-rate)

    def respond(b, state):
        weighted = reading * (starts[b] + state)
        rows = [jnp.sum(modes[j] * weighted, axis=0, keepdims=True) for j in range(NODES)]
        rows += [jnp.zeros_like(rows[0])] * (ROWS - NODES)
        answer = jnp.concatenate(rows, axis=0).astype(bf16)

        @pl.when(b != me)
        def _():
            h_send[b] = answer
            h_copy(b, me).start()

        @pl.when(b == me)
        def _():
            h_recv[me] = answer

        return block_decay * state

    lax.fori_loop(0, members, respond, entering)

    @pl.loop(early, members)
    def _(i):
        own_part(i)

    loads[10].wait()

    @pl.loop(0, members)
    def _(i):
        at = other(i)
        @pl.when(i > 0)
        def _():
            h_copy(at, at).wait_recv()

        for k, cols in enumerate(strips(at)):
            answer = h_recv[at, :, k * LANES:(k + 1) * LANES]
            carried = jnp.dot(basis[...], answer, preferred_element_type=f32)
            conv = (y[:, cols] + carried).astype(bf16)
            out[:, cols] = (gate[:, cols].astype(f32) * conv.astype(f32)).astype(bf16)

    @pl.when(position < total - 1)
    def _():
        b_copy.wait_send()

    @pl.loop(1, members)
    def _(i):
        g_copy(other(i), me).wait_send()
        m_copy(other(i), me).wait_send()
        h_copy(other(i), me).wait_send()

    @pl.loop(plane + 1, planes)
    def _(i):
        z_copy(i, plane).wait_send()


def local(n_seq, n_chan, features, short_weight, decay_rate, residue, skip_gain):
    streams, block, width = features.shape
    modes = decay_rate.shape[0]
    cores = 2 if n_seq % 2 == 0 else 1
    members = n_chan * cores
    planes = n_seq // cores
    own_width = width // members
    halo = streams * (short_weight.shape[1] - 1)
    fold = width // 4
    halo_rows = -(-halo * 4 // 16) * 16
    toeplitz, moment, basis = constant_tables(block)
    anywhere = pl.BlockSpec(memory_space=pl.ANY)
    dma = pltpu.SemaphoreType.DMA
    small = pltpu.VMEM((members, ROWS, own_width), bf16)
    return pl.pallas_call(
        functools.partial(kernel, n_seq, n_chan, cores),
        out_shape=pltpu.VMEM((block, width), bf16),
        in_specs=[anywhere] * 8,
        out_specs=pl.BlockSpec(memory_space=pltpu.VMEM),
        scratch_shapes=[
            pltpu.VMEM((streams, block, width), bf16),
            pltpu.VMEM((streams, 16, width), bf16),
            pltpu.VMEM(short_weight.shape, f32),
            pltpu.VMEM((modes, own_width), f32),
            pltpu.VMEM((modes, own_width), f32),
            pltpu.VMEM((1, own_width), f32),
            pltpu.VMEM(toeplitz.shape, bf16),
            pltpu.VMEM(moment.shape, bf16),
            pltpu.VMEM(basis.shape, bf16),
            pltpu.VMEM((block, width), bf16),
            pltpu.VMEM((block, width), bf16),
            pltpu.VMEM((block, width), f32),
            pltpu.VMEM((NODES * block, own_width), bf16),
            pltpu.VMEM((NODES, modes, own_width), f32),
            pltpu.VMEM((members, modes, own_width), f32),
            pltpu.VMEM((-(-halo // 8) * 8, width), f32),
            pltpu.VMEM((halo_rows, fold), bf16),
            pltpu.VMEM((halo_rows, fold), bf16),
            small, small, small,
            pltpu.VMEM((modes, own_width), bf16),
            pltpu.VMEM((planes, modes, own_width), bf16),
            small, small,
            dma((11,)), dma, dma,
            dma((members,)), dma((members,)), dma((members,)), dma((members,)),
            dma((members,)), dma((members,)), dma((planes,)), dma((planes,)),
        ],
        compiler_params=pltpu.CompilerParams(
            collective_id=0, has_side_effects=True, vmem_limit_bytes=60 * 2**20),
        cost_estimate=pl.CostEstimate(
            flops=2 * block * NODES * block * width,
            bytes_accessed=8 * block * width, transcendentals=0),
    )(
        features, short_weight, decay_rate, residue, skip_gain.reshape(1, -1),
        jnp.asarray(toeplitz, bf16), jnp.asarray(moment, bf16), jnp.asarray(basis, bf16),
    )


def solution(mesh):
    return jax.shard_map(
        functools.partial(local, mesh.shape["seq"], mesh.shape["chan"]),
        mesh=mesh,
        in_specs=(P(None, ("seq", "chan"), None), P(), P(None, "chan"), P(None, "chan"), P("chan")),
        out_specs=P(("seq", "chan"), None),
        check_vma=False,
    )
```

```python
import functools

import jax
import jax.numpy as jnp
import numpy as np
from jax import lax
from jax.experimental import pallas as pl
from jax.experimental.pallas import tpu as pltpu
from jax.sharding import PartitionSpec as P

MESH = pl.DeviceIdType.MESH
f32, bf16 = jnp.float32, jnp.bfloat16

NODES = 12
ROWS = 16
LANES = 128


def node_places(block):
    j = np.arange(NODES)
    return (block - 1) / 2 * (1 - np.cos(np.pi * (2 * j + 1) / (2 * NODES)))


def cardinals(points, nodes):
    out = np.ones((NODES,) + points.shape)
    for j in range(NODES):
        for i in range(NODES):
            if i != j:
                out[j] *= (points - nodes[i]) / (nodes[j] - nodes[i])
    return out


def constant_tables(block):
    nodes = node_places(block)
    t = np.arange(block)
    lag = t[:, None] - t[None, :]
    toeplitz = np.where(lag >= 0, cardinals(np.abs(lag).astype(float), nodes), 0.0)
    toeplitz = toeplitz.transpose(1, 0, 2).reshape(block, NODES * block)
    basis = np.zeros((block, ROWS))
    basis[:, :NODES] = cardinals(t.astype(float), nodes).T
    moment = basis[::-1].T
    return toeplitz, moment, basis


def kernel(
    n_seq, n_chan, cores, feat_hbm, taps_hbm, decay_hbm, residue_hbm, skip_hbm, toeplitz_hbm,
    moment_hbm, basis_hbm, out,
    feat, tail, taps, decay, residue, skip, toeplitz, moment, basis, prod, gate, y, gx, modes, starts, border, b_send, b_recv,
    g_all, m_send, m_recv, z_send, z_recv, h_send, h_recv,
    load_sem, b_ss, b_rs, g_ss, g_rs, m_ss, m_rs, h_ss, h_rs, z_ss, z_rs,
):
    streams, block, width = feat.shape
    n_taps = taps.shape[1]
    members = n_chan * cores
    planes = n_seq // cores
    own_width = width // members
    chan_width = width // n_chan
    fold = b_send.shape[1]
    folds = width // fold
    nodes = [float(v) for v in node_places(block)]

    seq, chan = lax.axis_index("seq"), lax.axis_index("chan")
    plane, core = seq // cores, lax.rem(seq, cores)
    me = core * n_chan + chan

    def member(i):
        return (plane * cores + i // n_chan, lax.rem(i, n_chan))

    def columns(i):
        start = lax.rem(i, n_chan) * chan_width + (i // n_chan) * own_width
        return pl.ds(pl.multiple_of(start, own_width), own_width)

    def strips(i):
        start = lax.rem(i, n_chan) * chan_width + (i // n_chan) * own_width
        for k in range(0, own_width, LANES):
            yield pl.ds(pl.multiple_of(start + k, LANES), LANES)

    def other(i):
        return lax.rem(me + i, members)

    own = pl.ds(pl.multiple_of(core * own_width, own_width), own_width)
    places = [
        (feat_hbm.at[:, pl.ds(block - 16, 16), :], tail),
        (decay_hbm.at[:, own], decay), (residue_hbm.at[:, own], residue),
        (skip_hbm.at[:, own], skip), (taps_hbm, taps),
        (feat_hbm.at[1], feat.at[1]), (feat_hbm.at[2], feat.at[2]),
        (moment_hbm, moment), (feat_hbm.at[0], feat.at[0]),
        (toeplitz_hbm, toeplitz), (basis_hbm, basis),
    ]
    loads = [pltpu.make_async_copy(a, b, load_sem.at[k]) for k, (a, b) in enumerate(places)]
    for load in loads:
        load.start()

    barrier = pltpu.get_barrier_semaphore()

    @pl.loop(1, members)
    def _(i):
        pl.semaphore_signal(barrier, inc=1, device_id=member(other(i)), device_id_type=MESH)

    @pl.loop(1, planes)
    def _(i):
        there = lax.rem(plane + i, planes) * cores + core
        pl.semaphore_signal(barrier, inc=1, device_id=(there, chan), device_id_type=MESH)

    enters = jnp.logical_and(me == 0, plane > 0)
    leaves = jnp.logical_and(me == members - 1, plane < planes - 1)

    @pl.when(enters)
    def _():
        pl.semaphore_signal(
            barrier, inc=1, device_id=(plane * cores - 1, n_chan - 1), device_id_type=MESH)

    @pl.when(leaves)
    def _():
        pl.semaphore_signal(
            barrier, inc=1, device_id=((plane + 1) * cores, 0), device_id_type=MESH)

    loads[0].wait()
    rows = []
    for m in range(streams):
        last = tail[m].astype(f32)
        for k in range(n_taps - 1):
            row = 16 - (n_taps - 1) + k
            rows += [last[row:row + 1, f * fold:(f + 1) * fold] for f in range(folds)]
    rows += [jnp.zeros_like(rows[0])] * (b_send.shape[0] - len(rows))
    b_send[...] = jnp.concatenate(rows, axis=0).astype(bf16)

    for load in loads[1:4]:
        load.wait()
    rate = decay[...]
    scaled = residue[...] * jnp.sqrt(1.0 - jnp.exp(-2.0 * rate))
    rows = []
    for j in range(NODES):
        a = jnp.exp(-rate * nodes[j])
        modes[j] = a
        rows.append(jnp.sum(scaled * a, axis=0, keepdims=True))
    gain = skip[...]
    gain_top = gain.astype(bf16).astype(f32)
    rows += [gain_top, gain - gain_top]
    rows += [jnp.zeros_like(gain)] * (ROWS - len(rows))
    g_all[me] = jnp.concatenate(rows, axis=0).astype(bf16)

    extra = jnp.where(enters, 1, 0) + jnp.where(leaves, 1, 0)
    pl.semaphore_wait(barrier, members - 1 + planes - 1 + extra)

    position = seq * n_chan + chan
    total = n_seq * n_chan
    after = lax.rem(position + 1, total)
    b_copy = pltpu.make_async_remote_copy(
        src_ref=b_send, dst_ref=b_recv, send_sem=b_ss, recv_sem=b_rs,
        device_id=(after // n_chan, lax.rem(after, n_chan)), device_id_type=MESH)

    @pl.when(position < total - 1)
    def _():
        b_copy.start()

    def g_copy(i, slot):
        return pltpu.make_async_remote_copy(
            src_ref=g_all.at[slot], dst_ref=g_all.at[slot], send_sem=g_ss.at[i],
            recv_sem=g_rs.at[slot], device_id=member(i), device_id_type=MESH)

    def m_copy(i, slot):
        return pltpu.make_async_remote_copy(
            src_ref=m_send.at[i], dst_ref=m_recv.at[slot], send_sem=m_ss.at[i],
            recv_sem=m_rs.at[slot], device_id=member(i), device_id_type=MESH)

    def h_copy(i, slot):
        return pltpu.make_async_remote_copy(
            src_ref=h_send.at[i], dst_ref=h_recv.at[slot], send_sem=h_ss.at[i],
            recv_sem=h_rs.at[slot], device_id=member(i), device_id_type=MESH)

    def z_copy(i, slot):
        return pltpu.make_async_remote_copy(
            src_ref=z_send, dst_ref=z_recv.at[slot], send_sem=z_ss.at[i],
            recv_sem=z_rs.at[slot], device_id=(i * cores + core, chan), device_id_type=MESH)

    @pl.loop(1, members)
    def _(i):
        g_copy(other(i), me).start()

    top_row = lax.broadcasted_iota(jnp.int32, (8, LANES), 0)

    def short_filter(m, cols, rows, with_border):
        x = feat[m, :rows, cols].astype(f32)
        total = taps[m, 0:1, cols] * x
        for j in range(1, n_taps):
            moved = pltpu.roll(x, j, 0)
            if with_border:
                top = moved[:8]
                for k in range(j):
                    place = m * (n_taps - 1) + n_taps - 1 - j + k
                    top = jnp.where(top_row == k, border[place:place + 1, cols], top)
                moved = jnp.concatenate([top, moved[8:]], axis=0)
            total = total + taps[m, j:j + 1, cols] * moved
        return total.astype(bf16)

    def product(cols, rows, with_border):
        left = short_filter(1, cols, rows, with_border).astype(f32)
        return (left * short_filter(2, cols, rows, with_border).astype(f32)).astype(bf16)

    for load in loads[4:7]:
        load.wait()

    @pl.loop(0, members)
    def _(i):
        for cols in strips(i):
            prod[:, cols] = product(cols, block, False)

    @pl.when(position > 0)
    def _():
        b_copy.wait_recv()
        got = b_recv[...].astype(f32)
        for m in range(streams):
            for k in range(n_taps - 1):
                for f in range(folds):
                    row = (m * (n_taps - 1) + k) * folds + f
                    border[m * (n_taps - 1) + k:m * (n_taps - 1) + k + 1,
                           f * fold:(f + 1) * fold] = got[row:row + 1]

    @pl.when(position == 0)
    def _():
        border[...] = jnp.zeros_like(border)

    loads[7].wait()

    @pl.loop(1, members + 1)
    def _(i):
        to = other(i)
        for cols in strips(to):
            prod[:16, cols] = product(cols, 16, True)
        found = jnp.dot(moment[...], prod[:, columns(to)], preferred_element_type=f32).astype(bf16)

        @pl.when(i < members)
        def _():
            m_send[to] = found
            m_copy(to, me).start()

        @pl.when(i == members)
        def _():
            m_recv[me] = found

    loads[8].wait()

    @pl.loop(0, members)
    def _(i):
        for cols in strips(i):
            gate[:, cols] = short_filter(0, cols, block, True)

    block_decay = jnp.exp(-rate * block)

    @pl.loop(1, members)
    def _(i):
        m_copy(other(i), other(i)).wait_recv()

    def gather_block(b, state):
        starts[b] = state
        found = m_recv[b].astype(f32)
        state = block_decay * state
        for j in range(NODES):
            state = state + modes[j] * found[j:j + 1]
        return state

    final = lax.fori_loop(0, members, gather_block, jnp.zeros_like(rate))
    z_send[...] = final.astype(bf16)

    @pl.loop(plane + 1, planes)
    def _(i):
        z_copy(i, plane).start()

    @pl.loop(1, members)
    def _(i):
        g_copy(other(i), other(i)).wait_recv()

    loads[9].wait()

    def own_part(i):
        cols = columns(i)
        p = prod[:, cols]
        g = g_all[i].astype(f32)
        for j in range(NODES):
            row = jnp.broadcast_to(g[j:j + 1], (16, own_width)).astype(bf16)
            for r in range(0, block, 16):
                gx[j * block + r:j * block + r + 16, :] = row * p[r:r + 16]
        inner = jnp.dot(toeplitz[...], gx[...], preferred_element_type=f32)
        both = g[NODES:NODES + 1] + g[NODES + 1:NODES + 2]
        y[:, cols] = inner + both * p.astype(f32)

    early = members // 2

    @pl.loop(0, early)
    def _(i):
        own_part(i)

    plane_decay = jnp.exp(-rate * (block * members))

    def gather_plane(i, state):
        z_copy(i, i).wait_recv()
        return plane_decay * state + z_recv[i].astype(f32)

    entering = lax.fori_loop(0, plane, gather_plane, jnp.zeros_like(rate))
    reading = scaled * jnp.exp(-rate)

    def respond(b, state):
        weighted = reading * (starts[b] + state)
        rows = [jnp.sum(modes[j] * weighted, axis=0, keepdims=True) for j in range(NODES)]
        rows += [jnp.zeros_like(rows[0])] * (ROWS - NODES)
        answer = jnp.concatenate(rows, axis=0).astype(bf16)

        @pl.when(b != me)
        def _():
            h_send[b] = answer
            h_copy(b, me).start()

        @pl.when(b == me)
        def _():
            h_recv[me] = answer

        return block_decay * state

    lax.fori_loop(0, members, respond, entering)

    @pl.loop(early, members)
    def _(i):
        own_part(i)

    loads[10].wait()

    @pl.loop(0, members)
    def _(i):
        at = other(i)
        @pl.when(i > 0)
        def _():
            h_copy(at, at).wait_recv()

        for k, cols in enumerate(strips(at)):
            answer = h_recv[at, :, k * LANES:(k + 1) * LANES]
            carried = jnp.dot(basis[...], answer, preferred_element_type=f32)
            conv = (y[:, cols] + carried).astype(bf16)
            out[:, cols] = (gate[:, cols].astype(f32) * conv.astype(f32)).astype(bf16)

    @pl.when(position < total - 1)
    def _():
        b_copy.wait_send()

    @pl.loop(1, members)
    def _(i):
        g_copy(other(i), me).wait_send()
        m_copy(other(i), me).wait_send()
        h_copy(other(i), me).wait_send()

    @pl.loop(plane + 1, planes)
    def _(i):
        z_copy(i, plane).wait_send()


def local(n_seq, n_chan, features, short_weight, decay_rate, residue, skip_gain):
    streams, block, width = features.shape
    modes = decay_rate.shape[0]
    cores = 2 if n_seq % 2 == 0 else 1
    members = n_chan * cores
    planes = n_seq // cores
    own_width = width // members
    halo = streams * (short_weight.shape[1] - 1)
    fold = width // 4
    halo_rows = -(-halo * 4 // 16) * 16
    toeplitz, moment, basis = constant_tables(block)
    anywhere = pl.BlockSpec(memory_space=pl.ANY)
    dma = pltpu.SemaphoreType.DMA
    small = pltpu.VMEM((members, ROWS, own_width), bf16)
    return pl.pallas_call(
        functools.partial(kernel, n_seq, n_chan, cores),
        out_shape=pltpu.VMEM((block, width), bf16),
        in_specs=[anywhere] * 8,
        out_specs=pl.BlockSpec(memory_space=pltpu.VMEM),
        scratch_shapes=[
            pltpu.VMEM((streams, block, width), bf16),
            pltpu.VMEM((streams, 16, width), bf16),
            pltpu.VMEM(short_weight.shape, f32),
            pltpu.VMEM((modes, own_width), f32),
            pltpu.VMEM((modes, own_width), f32),
            pltpu.VMEM((1, own_width), f32),
            pltpu.VMEM(toeplitz.shape, bf16),
            pltpu.VMEM(moment.shape, bf16),
            pltpu.VMEM(basis.shape, bf16),
            pltpu.VMEM((block, width), bf16),
            pltpu.VMEM((block, width), bf16),
            pltpu.VMEM((block, width), f32),
            pltpu.VMEM((NODES * block, own_width), bf16),
            pltpu.VMEM((NODES, modes, own_width), f32),
            pltpu.VMEM((members, modes, own_width), f32),
            pltpu.VMEM((-(-halo // 8) * 8, width), f32),
            pltpu.VMEM((halo_rows, fold), bf16),
            pltpu.VMEM((halo_rows, fold), bf16),
            small, small, small,
            pltpu.VMEM((modes, own_width), bf16),
            pltpu.VMEM((planes, modes, own_width), bf16),
            small, small,
            dma((11,)), dma, dma,
            dma((members,)), dma((members,)), dma((members,)), dma((members,)),
            dma((members,)), dma((members,)), dma((planes,)), dma((planes,)),
        ],
        compiler_params=pltpu.CompilerParams(
            collective_id=0, has_side_effects=True, vmem_limit_bytes=60 * 2**20),
        cost_estimate=pl.CostEstimate(
            flops=2 * block * NODES * block * width,
            bytes_accessed=8 * block * width, transcendentals=0),
    )(
        features, short_weight, decay_rate, residue, skip_gain.reshape(1, -1),
        jnp.asarray(toeplitz, bf16), jnp.asarray(moment, bf16), jnp.asarray(basis, bf16),
    )


def solution(mesh):
    return jax.shard_map(
        functools.partial(local, mesh.shape["seq"], mesh.shape["chan"]),
        mesh=mesh,
        in_specs=(P(None, ("seq", "chan"), None), P(), P(None, "chan"), P(None, "chan"), P("chan")),
        out_specs=P(("seq", "chan"), None),
        check_vma=False,
    )
```

```python
import functools

import jax
import jax.numpy as jnp
import numpy as np
from jax import lax
from jax.experimental import pallas as pl
from jax.experimental.pallas import tpu as pltpu
from jax.sharding import PartitionSpec as P

MESH = pl.DeviceIdType.MESH
f32, bf16 = jnp.float32, jnp.bfloat16

NODES = 12
ROWS = 16
LANES = 128


def node_places(block):
    j = np.arange(NODES)
    return (block - 1) / 2 * (1 - np.cos(np.pi * (2 * j + 1) / (2 * NODES)))


def cardinals(points, nodes):
    out = np.ones((NODES,) + points.shape)
    for j in range(NODES):
        for i in range(NODES):
            if i != j:
                out[j] *= (points - nodes[i]) / (nodes[j] - nodes[i])
    return out


def constant_tables(block):
    nodes = node_places(block)
    t = np.arange(block)
    lag = t[:, None] - t[None, :]
    toeplitz = np.where(lag >= 0, cardinals(np.abs(lag).astype(float), nodes), 0.0)
    toeplitz = toeplitz.transpose(1, 0, 2).reshape(block, NODES * block)
    basis = np.zeros((block, ROWS))
    basis[:, :NODES] = cardinals(t.astype(float), nodes).T
    moment = basis[::-1].T
    return toeplitz, moment, basis


def kernel(
    n_seq, n_chan, cores, feat_hbm, taps_hbm, decay_hbm, residue_hbm, skip_hbm, toeplitz_hbm,
    moment_hbm, basis_hbm, out,
    feat, tail, taps, decay, residue, skip, toeplitz, moment, basis, prod, gate, y, gx, modes, starts, border, b_send, b_recv,
    g_all, m_send, m_recv, z_send, z_recv, h_send, h_recv,
    load_sem, b_ss, b_rs, g_ss, g_rs, m_ss, m_rs, h_ss, h_rs, z_ss, z_rs,
):
    streams, block, width = feat.shape
    n_taps = taps.shape[1]
    members = n_chan * cores
    planes = n_seq // cores
    own_width = width // members
    chan_width = width // n_chan
    fold = b_send.shape[1]
    folds = width // fold
    nodes = [float(v) for v in node_places(block)]

    seq, chan = lax.axis_index("seq"), lax.axis_index("chan")
    plane, core = seq // cores, lax.rem(seq, cores)
    me = core * n_chan + chan

    def member(i):
        return (plane * cores + i // n_chan, lax.rem(i, n_chan))

    def columns(i):
        start = lax.rem(i, n_chan) * chan_width + (i // n_chan) * own_width
        return pl.ds(pl.multiple_of(start, own_width), own_width)

    def strips(i):
        start = lax.rem(i, n_chan) * chan_width + (i // n_chan) * own_width
        for k in range(0, own_width, LANES):
            yield pl.ds(pl.multiple_of(start + k, LANES), LANES)

    def other(i):
        return lax.rem(me + i, members)

    own = pl.ds(pl.multiple_of(core * own_width, own_width), own_width)
    places = [
        (feat_hbm.at[:, pl.ds(block - 16, 16), :], tail),
        (decay_hbm.at[:, own], decay), (residue_hbm.at[:, own], residue),
        (skip_hbm.at[:, own], skip), (taps_hbm, taps),
        (feat_hbm.at[1], feat.at[1]), (feat_hbm.at[2], feat.at[2]),
        (moment_hbm, moment), (feat_hbm.at[0], feat.at[0]),
        (toeplitz_hbm, toeplitz), (basis_hbm, basis),
    ]
    loads = [pltpu.make_async_copy(a, b, load_sem.at[k]) for k, (a, b) in enumerate(places)]
    for load in loads:
        load.start()

    barrier = pltpu.get_barrier_semaphore()

    @pl.loop(1, members)
    def _(i):
        pl.semaphore_signal(barrier, inc=1, device_id=member(other(i)), device_id_type=MESH)

    @pl.loop(1, planes)
    def _(i):
        there = lax.rem(plane + i, planes) * cores + core
        pl.semaphore_signal(barrier, inc=1, device_id=(there, chan), device_id_type=MESH)

    enters = jnp.logical_and(me == 0, plane > 0)
    leaves = jnp.logical_and(me == members - 1, plane < planes - 1)

    @pl.when(enters)
    def _():
        pl.semaphore_signal(
            barrier, inc=1, device_id=(plane * cores - 1, n_chan - 1), device_id_type=MESH)

    @pl.when(leaves)
    def _():
        pl.semaphore_signal(
            barrier, inc=1, device_id=((plane + 1) * cores, 0), device_id_type=MESH)

    loads[0].wait()
    rows = []
    for m in range(streams):
        last = tail[m].astype(f32)
        for k in range(n_taps - 1):
            row = 16 - (n_taps - 1) + k
            rows += [last[row:row + 1, f * fold:(f + 1) * fold] for f in range(folds)]
    rows += [jnp.zeros_like(rows[0])] * (b_send.shape[0] - len(rows))
    b_send[...] = jnp.concatenate(rows, axis=0).astype(bf16)

    for load in loads[1:4]:
        load.wait()
    rate = decay[...]
    scaled = residue[...] * jnp.sqrt(1.0 - jnp.exp(-2.0 * rate))
    rows = []
    for j in range(NODES):
        a = jnp.exp(-rate * nodes[j])
        modes[j] = a
        rows.append(jnp.sum(scaled * a, axis=0, keepdims=True))
    gain = skip[...]
    gain_top = gain.astype(bf16).astype(f32)
    rows += [gain_top, gain - gain_top]
    rows += [jnp.zeros_like(gain)] * (ROWS - len(rows))
    g_all[me] = jnp.concatenate(rows, axis=0).astype(bf16)

    top_row = lax.broadcasted_iota(jnp.int32, (8, LANES), 0)

    def short_filter(m, cols, rows, with_border):
        x = feat[m, :rows, cols].astype(f32)
        total = taps[m, 0:1, cols] * x
        for j in range(1, n_taps):
            moved = pltpu.roll(x, j, 0)
            if with_border:
                top = moved[:8]
                for k in range(j):
                    place = m * (n_taps - 1) + n_taps - 1 - j + k
                    top = jnp.where(top_row == k, border[place:place + 1, cols], top)
                moved = jnp.concatenate([top, moved[8:]], axis=0)
            total = total + taps[m, j:j + 1, cols] * moved
        return total.astype(bf16)

    def product(cols, rows, with_border):
        left = short_filter(1, cols, rows, with_border).astype(f32)
        return (left * short_filter(2, cols, rows, with_border).astype(f32)).astype(bf16)

    for load in loads[4:7]:
        load.wait()

    half = members // 2

    @pl.loop(0, half)
    def _(i):
        for cols in strips(i):
            prod[:, cols] = product(cols, block, False)

    extra = jnp.where(enters, 1, 0) + jnp.where(leaves, 1, 0)
    pl.semaphore_wait(barrier, members - 1 + planes - 1 + extra)

    position = seq * n_chan + chan
    total = n_seq * n_chan
    after = lax.rem(position + 1, total)
    b_copy = pltpu.make_async_remote_copy(
        src_ref=b_send, dst_ref=b_recv, send_sem=b_ss, recv_sem=b_rs,
        device_id=(after // n_chan, lax.rem(after, n_chan)), device_id_type=MESH)

    @pl.when(position < total - 1)
    def _():
        b_copy.start()

    def g_copy(i, slot):
        return pltpu.make_async_remote_copy(
            src_ref=g_all.at[slot], dst_ref=g_all.at[slot], send_sem=g_ss.at[i],
            recv_sem=g_rs.at[slot], device_id=member(i), device_id_type=MESH)

    def m_copy(i, slot):
        return pltpu.make_async_remote_copy(
            src_ref=m_send.at[i], dst_ref=m_recv.at[slot], send_sem=m_ss.at[i],
            recv_sem=m_rs.at[slot], device_id=member(i), device_id_type=MESH)

    def h_copy(i, slot):
        return pltpu.make_async_remote_copy(
            src_ref=h_send.at[i], dst_ref=h_recv.at[slot], send_sem=h_ss.at[i],
            recv_sem=h_rs.at[slot], device_id=member(i), device_id_type=MESH)

    def z_copy(i, slot):
        return pltpu.make_async_remote_copy(
            src_ref=z_send, dst_ref=z_recv.at[slot], send_sem=z_ss.at[i],
            recv_sem=z_rs.at[slot], device_id=(i * cores + core, chan), device_id_type=MESH)

    @pl.loop(1, members)
    def _(i):
        g_copy(other(i), me).start()

    @pl.loop(half, members)
    def _(i):
        for cols in strips(i):
            prod[:, cols] = product(cols, block, False)

    @pl.when(position > 0)
    def _():
        b_copy.wait_recv()
        got = b_recv[...].astype(f32)
        for m in range(streams):
            for k in range(n_taps - 1):
                for f in range(folds):
                    row = (m * (n_taps - 1) + k) * folds + f
                    border[m * (n_taps - 1) + k:m * (n_taps - 1) + k + 1,
                           f * fold:(f + 1) * fold] = got[row:row + 1]

    @pl.when(position == 0)
    def _():
        border[...] = jnp.zeros_like(border)

    loads[7].wait()

    @pl.loop(1, members + 1)
    def _(i):
        to = other(i)
        for cols in strips(to):
            prod[:16, cols] = product(cols, 16, True)
        found = jnp.dot(moment[...], prod[:, columns(to)], preferred_element_type=f32).astype(bf16)

        @pl.when(i < members)
        def _():
            m_send[to] = found
            m_copy(to, me).start()

        @pl.when(i == members)
        def _():
            m_recv[me] = found

    loads[8].wait()

    @pl.loop(0, members)
    def _(i):
        for cols in strips(i):
            gate[:, cols] = short_filter(0, cols, block, True)

    block_decay = jnp.exp(-rate * block)

    @pl.loop(1, members)
    def _(i):
        m_copy(other(i), other(i)).wait_recv()

    def gather_block(b, state):
        starts[b] = state
        found = m_recv[b].astype(f32)
        state = block_decay * state
        for j in range(NODES):
            state = state + modes[j] * found[j:j + 1]
        return state

    final = lax.fori_loop(0, members, gather_block, jnp.zeros_like(rate))
    z_send[...] = final.astype(bf16)

    @pl.loop(plane + 1, planes)
    def _(i):
        z_copy(i, plane).start()

    @pl.loop(1, members)
    def _(i):
        g_copy(other(i), other(i)).wait_recv()

    loads[9].wait()

    def own_part(i):
        cols = columns(i)
        p = prod[:, cols]
        g = g_all[i].astype(f32)
        for j in range(NODES):
            row = jnp.broadcast_to(g[j:j + 1], (16, own_width)).astype(bf16)
            for r in range(0, block, 16):
                gx[j * block + r:j * block + r + 16, :] = row * p[r:r + 16]
        inner = jnp.dot(toeplitz[...], gx[...], preferred_element_type=f32)
        both = g[NODES:NODES + 1] + g[NODES + 1:NODES + 2]
        y[:, cols] = inner + both * p.astype(f32)

    early = members // 2

    @pl.loop(0, early)
    def _(i):
        own_part(i)

    plane_decay = jnp.exp(-rate * (block * members))

    def gather_plane(i, state):
        z_copy(i, i).wait_recv()
        return plane_decay * state + z_recv[i].astype(f32)

    entering = lax.fori_loop(0, plane, gather_plane, jnp.zeros_like(rate))
    reading = scaled * jnp.exp(-rate)

    def respond(b, state):
        weighted = reading * (starts[b] + state)
        rows = [jnp.sum(modes[j] * weighted, axis=0, keepdims=True) for j in range(NODES)]
        rows += [jnp.zeros_like(rows[0])] * (ROWS - NODES)
        answer = jnp.concatenate(rows, axis=0).astype(bf16)

        @pl.when(b != me)
        def _():
            h_send[b] = answer
            h_copy(b, me).start()

        @pl.when(b == me)
        def _():
            h_recv[me] = answer

        return block_decay * state

    lax.fori_loop(0, members, respond, entering)

    @pl.loop(early, members)
    def _(i):
        own_part(i)

    loads[10].wait()

    @pl.loop(0, members)
    def _(i):
        at = other(i)
        @pl.when(i > 0)
        def _():
            h_copy(at, at).wait_recv()

        for k, cols in enumerate(strips(at)):
            answer = h_recv[at, :, k * LANES:(k + 1) * LANES]
            carried = jnp.dot(basis[...], answer, preferred_element_type=f32)
            conv = (y[:, cols] + carried).astype(bf16)
            out[:, cols] = (gate[:, cols].astype(f32) * conv.astype(f32)).astype(bf16)

    @pl.when(position < total - 1)
    def _():
        b_copy.wait_send()

    @pl.loop(1, members)
    def _(i):
        g_copy(other(i), me).wait_send()
        m_copy(other(i), me).wait_send()
        h_copy(other(i), me).wait_send()

    @pl.loop(plane + 1, planes)
    def _(i):
        z_copy(i, plane).wait_send()


def local(n_seq, n_chan, features, short_weight, decay_rate, residue, skip_gain):
    streams, block, width = features.shape
    modes = decay_rate.shape[0]
    cores = 2 if n_seq % 2 == 0 else 1
    members = n_chan * cores
    planes = n_seq // cores
    own_width = width // members
    halo = streams * (short_weight.shape[1] - 1)
    fold = width // 4
    halo_rows = -(-halo * 4 // 16) * 16
    toeplitz, moment, basis = constant_tables(block)
    anywhere = pl.BlockSpec(memory_space=pl.ANY)
    dma = pltpu.SemaphoreType.DMA
    small = pltpu.VMEM((members, ROWS, own_width), bf16)
    return pl.pallas_call(
        functools.partial(kernel, n_seq, n_chan, cores),
        out_shape=pltpu.VMEM((block, width), bf16),
        in_specs=[anywhere] * 8,
        out_specs=pl.BlockSpec(memory_space=pltpu.VMEM),
        scratch_shapes=[
            pltpu.VMEM((streams, block, width), bf16),
            pltpu.VMEM((streams, 16, width), bf16),
            pltpu.VMEM(short_weight.shape, f32),
            pltpu.VMEM((modes, own_width), f32),
            pltpu.VMEM((modes, own_width), f32),
            pltpu.VMEM((1, own_width), f32),
            pltpu.VMEM(toeplitz.shape, bf16),
            pltpu.VMEM(moment.shape, bf16),
            pltpu.VMEM(basis.shape, bf16),
            pltpu.VMEM((block, width), bf16),
            pltpu.VMEM((block, width), bf16),
            pltpu.VMEM((block, width), f32),
            pltpu.VMEM((NODES * block, own_width), bf16),
            pltpu.VMEM((NODES, modes, own_width), f32),
            pltpu.VMEM((members, modes, own_width), f32),
            pltpu.VMEM((-(-halo // 8) * 8, width), f32),
            pltpu.VMEM((halo_rows, fold), bf16),
            pltpu.VMEM((halo_rows, fold), bf16),
            small, small, small,
            pltpu.VMEM((modes, own_width), bf16),
            pltpu.VMEM((planes, modes, own_width), bf16),
            small, small,
            dma((11,)), dma, dma,
            dma((members,)), dma((members,)), dma((members,)), dma((members,)),
            dma((members,)), dma((members,)), dma((planes,)), dma((planes,)),
        ],
        compiler_params=pltpu.CompilerParams(
            collective_id=0, has_side_effects=True, vmem_limit_bytes=60 * 2**20),
        cost_estimate=pl.CostEstimate(
            flops=2 * block * NODES * block * width,
            bytes_accessed=8 * block * width, transcendentals=0),
    )(
        features, short_weight, decay_rate, residue, skip_gain.reshape(1, -1),
        jnp.asarray(toeplitz, bf16), jnp.asarray(moment, bf16), jnp.asarray(basis, bf16),
    )


def solution(mesh):
    return jax.shard_map(
        functools.partial(local, mesh.shape["seq"], mesh.shape["chan"]),
        mesh=mesh,
        in_specs=(P(None, ("seq", "chan"), None), P(), P(None, "chan"), P(None, "chan"), P("chan")),
        out_specs=P(("seq", "chan"), None),
        check_vma=False,
    )
```
